32 devices in a mesh: section: 2 (over y), node: 4 (over z), local: 4 (over x, core).
Axes of the slice: x: 2, y: 2, z: 4, core: 2. Of those that a mesh axis runs over, the one named last changes fastest.
Arguments:
- prev_rows: bfloat16 [2, 2048, 3584], P('section', ('node', 'local')), may hold values from -6 to 6
- expert_ids: int32 [2, 2048, 1], P('section', ('node', 'local')), may hold values from 0 to 3; in each aligned block of 128 rows (0 to 127, 128 to 255, ..., all dimensions but the last counted through in order) at most 40 rows name the same one
- route_weight: float32 [2, 2048, 1], P('section', ('node', 'local')), may hold values from 0.3 to 1.5
- norm_gain: float32 [2, 3584], P('section'), may hold values from 0.1 to 1.9
- gate_weight: bfloat16 [2, 4, 3584, 1024], P('section', 'node', None, 'local'), may hold values from -0.09375 to 0.09375
- up_weight: bfloat16 [2, 4, 3584, 1024], P('section', 'node', None, 'local'), may hold values from -0.09375 to 0.09375
- down_weight: bfloat16 [2, 4, 1024, 3584], P('section', 'node', None, 'local'), may hold values from -0.1875 to 0.1875
Outputs:
- mixed: bfloat16 [2, 2048, 3584], P('section', ('node', 'local'))
The draws below stay inside these ranges and needn't reach their ends.
Inputs may be any that keep to these rules, and one draw needn't show every extreme that they name: `expert_ids`: within the 128 tokens of one device no expert is named more than 40 times, and the rows of some device name some expert exactly 40 times.
All inputs are finite; a program needn't handle non-finite values.
Results may differ from the reference program's by a relative error of at most 0.0051.
Values may be sent and summed in bfloat16 or wider, within the bound.
A program may use at most 64 MiB of HBM per device.

```python
import math
import jax
import jax.numpy as jnp
import numpy as np
from jax import lax

D = 3584
FF = 1024
TOP = 1
TOK_DEV = 128
EXPERTS = 4
CAP = 40
TG = 2048
N_SECTION = 2


def levels(stream_key, shape, pieces, least, top_value):
    factor_of, own = 1.0, jax.random.fold_in(stream_key, 6)
    for dim, blocks in pieces:
        draws = jnp.exp(jax.random.uniform(jax.random.fold_in(own, dim), (blocks,), jnp.float32, least / len(pieces), top_value / len(pieces)))
        factor_of = factor_of * jnp.repeat(draws, shape[dim] // blocks).reshape([-1 if axis == dim else 1 for axis in range(len(shape))])
    return factor_of


def routed_block(rng, own, number, rows, amount, top, most, skew):
    ranking = jax.random.permutation(rng, amount)
    crowded, usual = portions_of(amount, rows * top, most, skew, True), portions_of(amount, rows * top, most, skew, False)
    places = jnp.arange(amount)

    def named(tallies, offset_by):
        used = int((tallies > 0).sum())
        fixed = max(1, used // 4)
        passed = fixed + (places - fixed + offset_by * (used - fixed)) % max(1, amount - fixed)
        return jnp.zeros((amount,), jnp.int32).at[ranking[jnp.where(places < fixed, places, passed)]].set(jnp.asarray(tallies, jnp.int32))

    tallies = jnp.where(number % 4 == 0, named(crowded, number // 4), named(usual, number - number // 4 - 1))
    mixed = jax.random.permutation(jax.random.fold_in(own, 3), amount)
    source_of, receiver = mixed[0:amount // 2 * 2:2], mixed[1:amount // 2 * 2:2]
    room = jnp.minimum(tallies[source_of] - 1, most - tallies[receiver]) // 2
    room = jnp.where((source_of == ranking[0]) | (receiver == ranking[0]) | (tallies[receiver] == 0), 0, jnp.maximum(room, 0))
    passed = jax.random.randint(jax.random.fold_in(own, 4), (amount // 2,), 0, 1 << 20) % (room + 1)
    tallies = tallies.at[source_of].add(-passed).at[receiver].add(passed)
    labels = jnp.searchsorted(jnp.cumsum(tallies), jnp.arange(rows * top), side="right").astype(jnp.int32)
    table = labels.reshape(top, rows).T
    table = table[jax.random.permutation(jax.random.fold_in(own, 1), rows)]
    offset_by = jax.random.randint(jax.random.fold_in(own, 2), (rows, 1), 0, top)
    return jnp.take_along_axis(table, (jnp.arange(top)[None, :] + offset_by) % top, axis=1)


def portions_of(count, total, bound, lean, full):
    loads = [(1 << 20) // math.isqrt(grade ** lean) + 1 for grade in range(1, count + 1)]
    largest = bound if full else min(bound, max(-(-total // count), total * loads[0] // sum(loads)))
    least = 1 if total - largest >= count - 1 else 0
    counts, surplus = [largest] + [least] * (count - 1), total - largest - least * (count - 1)
    while surplus > 0:
        movable = [i for i in range(1, count) if counts[i] < largest] or [i for i in range(1, count) if counts[i] < bound]
        whole, budget = sum([loads[i] for i in movable]), surplus
        for i in movable:
            more = min(bound - counts[i], max(1, budget * loads[i] // whole), surplus)
            counts[i] = counts[i] + more
            surplus = surplus - more
    return np.array(counts)


def scatter_about(rng, extent, spread, reach, pieces=(), kind=jnp.bfloat16):
    factor_of = levels(rng, extent, pieces, -0.22, 0.18) if pieces else 1.0
    entries = jax.random.normal(rng, extent, jnp.float32) * spread * factor_of
    return jnp.minimum(jnp.maximum(entries, -reach), reach).astype(kind)


def setup_inputs(seed: int = 0) -> dict:
    seeds = jax.random.split(jax.random.key(seed), 8)
    prev_rows = scatter_about(seeds[0], (N_SECTION, TG, D), 1.0, 6.0, ((0, 2), (1, 16)))
    expert_ids_keys = jax.random.split(jax.random.fold_in(seeds[1], 1), N_SECTION * TG // TOK_DEV)
    expert_ids_turns = jax.random.permutation(jax.random.fold_in(seeds[1], 3), N_SECTION * TG // TOK_DEV)
    expert_ids = jax.vmap(lambda own, number: routed_block(jax.random.fold_in(seeds[1], 2), own, number, TOK_DEV, EXPERTS, TOP, CAP, 2))(expert_ids_keys, expert_ids_turns).reshape((N_SECTION, TG, TOP))
    route_weight = jnp.clip(0.3 + 1.2 * jax.random.uniform(seeds[2], (N_SECTION, TG, TOP), jnp.float32) ** levels(seeds[2], (N_SECTION, TG, TOP), ((0, 2), (1, 16)), -0.2, 0.2), 0.3, 1.5)
    norm_gain = jnp.clip(1.0 + 0.18 * jax.random.normal(seeds[3], (N_SECTION, D), jnp.float32), 0.1, 1.9)
    gate_weight = scatter_about(seeds[4], (N_SECTION, EXPERTS, D, FF), D ** -0.5, 0.09375, ((0, 2), (1, 4), (3, 4)))
    up_weight = scatter_about(seeds[5], (N_SECTION, EXPERTS, D, FF), D ** -0.5, 0.09375, ((0, 2), (1, 4), (3, 4)))
    down_weight = scatter_about(seeds[6], (N_SECTION, EXPERTS, FF, D), FF ** -0.5, 0.1875, ((0, 2), (1, 4), (3, 4)))
    return dict(prev_rows=prev_rows, expert_ids=expert_ids, route_weight=route_weight, norm_gain=norm_gain, gate_weight=gate_weight, up_weight=up_weight, down_weight=down_weight)


def expert_pass(inputs, w_gate, w_up, w_down):
    gate = jnp.dot(inputs, w_gate, preferred_element_type=jnp.float32)
    upper = jnp.dot(inputs, w_up, preferred_element_type=jnp.float32)
    hidden = (jax.nn.silu(gate) * upper).astype(jnp.bfloat16)
    return jnp.dot(hidden, w_down, preferred_element_type=jnp.float32).astype(jnp.bfloat16)

def reference(prev_rows, expert_ids, route_weight, norm_gain, gate_weight, up_weight, down_weight):
    shifted = jnp.roll(prev_rows, 1, axis=0)
    total = shifted.shape[1]
    feature = shifted.shape[2]
    blocks = total // TOK_DEV

    def one_section(packed):
        rows_s, ids_s, weight_s, gain_s, gate_s, up_s, down_s = packed
        wide = rows_s.astype(jnp.float32)
        scale = lax.rsqrt(lax.optimization_barrier(jnp.mean(wide * wide, axis=-1, keepdims=True)) + 1e-06)
        normed = (wide * scale * gain_s).astype(jnp.bfloat16)
        flat_ids = ids_s.reshape(blocks, TOK_DEV * TOP).astype(jnp.int32)
        onehot = (flat_ids[..., None] == jnp.arange(EXPERTS, dtype=jnp.int32)).astype(jnp.int32)
        slot = lax.optimization_barrier(jnp.sum((jnp.cumsum(onehot, axis=1) - onehot) * onehot, axis=2)).astype(jnp.int32)
        target = (flat_ids * CAP + slot).astype(jnp.int32)
        source = jnp.repeat(normed.reshape(blocks, TOK_DEV, feature), TOP, axis=1)

        def place(where, values):
            return jnp.zeros((EXPERTS * CAP, feature), jnp.bfloat16).at[where].set(values)
        dispatched = jax.vmap(place)(target, source).reshape(blocks, EXPERTS, CAP, feature)

        def one_expert(index):
            inputs = jnp.take(dispatched, index, axis=1).reshape(blocks * CAP, feature)
            return expert_pass(inputs, gate_s[index], up_s[index], down_s[index])
        outputs = lax.map(one_expert, jnp.arange(EXPERTS, dtype=jnp.int32))
        outputs = outputs.reshape(EXPERTS, blocks, CAP, feature).transpose(1, 0, 2, 3)
        outputs = outputs.reshape(blocks, EXPERTS * CAP, feature)
        picked = jax.vmap(lambda table, where: table[where])(outputs, target)
        picked = picked.astype(jnp.float32).reshape(total, TOP, feature)
        combined = lax.optimization_barrier(jnp.sum(picked * weight_s[..., None], axis=1))
        return (wide + combined).astype(jnp.bfloat16)
    return lax.map(one_section, (shifted, expert_ids, route_weight, norm_gain, gate_weight, up_weight, down_weight))
```

```python
import functools

import jax
import jax.numpy as jnp
from jax import lax
from jax.experimental import pallas as pl
from jax.experimental.pallas import tpu as pltpu
from jax.sharding import PartitionSpec as P

MESH = pl.DeviceIdType.MESH
HALVES = 2
CHUNK = 512


def kernel(
    sections, experts, members, slots,
    prev, ids, weight, gain, w_gate, w_up, w_down, out,
    rows, scale_out, scale_in, sel, sel_t, packed, arrived, w_in, w_out, total, hidden, results, returned,
    w_sem, y_send, y_recv, z_send, z_recv, g_send, g_recv, f_send, f_recv,
    h_send, h_recv, k_send, k_recv, r_send, r_recv,
):
    s, n, l = lax.axis_index("section"), lax.axis_index("node"), lax.axis_index("local")
    tokens, feature = prev.shape
    chunks = feature // CHUNK
    part = CHUNK // HALVES
    units = w_gate.shape[1]
    width = w_down.shape[1]
    tiles = -(-width // 128)
    ends = [min(128, width - 128 * t) for t in range(tiles)]
    group = members * slots
    chips = members // 2
    sibling = l + 1 - 2 * lax.rem(l, 2)
    order = sorted(range(experts), key=lambda k: -min(k, experts - k))

    loads = [
        pltpu.make_async_copy(w_gate, w_in.at[:, pl.ds(0, units)], w_sem.at[0]),
        pltpu.make_async_copy(w_up, w_in.at[:, pl.ds(units, units)], w_sem.at[1]),
        pltpu.make_async_copy(w_down, w_out, w_sem.at[2]),
    ]
    for load in loads:
        load.start()

    barrier = pltpu.get_barrier_semaphore()
    after, before = lax.rem(s + 1, sections), lax.rem(s + sections - 1, sections)
    for other in (after, before):
        pl.semaphore_signal(barrier, inc=1, device_id={"section": other, "node": n, "local": l}, device_id_type=MESH)
    for k in range(experts):
        for m in range(members):
            if k or m:
                place = {"section": s, "node": lax.rem(n + k, experts), "local": lax.rem(l + m, members)}
                pl.semaphore_signal(barrier, inc=1, device_id=place, device_id_type=MESH)

    wide = prev[...].astype(jnp.float32)
    mean = jnp.sum(wide * wide, axis=1, keepdims=True) / feature
    scale_out[...] = jnp.broadcast_to(lax.rsqrt(mean + 1e-06), scale_out.shape)

    chosen = ids[...]
    lanes = lax.broadcasted_iota(jnp.int32, (tokens, 128), 1)
    onehot = jnp.where(chosen == lanes, 1.0, 0.0)
    earlier = lax.broadcasted_iota(jnp.int32, (tokens, tokens), 1) < lax.broadcasted_iota(jnp.int32, (tokens, tokens), 0)
    counts = jnp.dot(
        jnp.where(earlier, 1.0, 0.0).astype(jnp.bfloat16), onehot.astype(jnp.bfloat16),
        preferred_element_type=jnp.float32,
    )
    slot = jnp.sum(counts * onehot, axis=1, keepdims=True)
    target = chosen.astype(jnp.float32) * slots + slot
    places = lax.broadcasted_iota(jnp.int32, (tokens, sel.shape[0]), 1).astype(jnp.float32)
    spread = jnp.where(target == places, 1.0, 0.0)
    sel_t[...] = spread.astype(jnp.bfloat16)
    sel[...] = spread.T.astype(jnp.bfloat16)
    total[...] = jnp.zeros_like(total)

    pl.semaphore_wait(barrier, experts * members + 1)

    def remote(src, dst, send, recv, **place):
        where = {"section": s, "node": n, "local": l}
        where.update(place)
        return pltpu.make_async_remote_copy(
            src_ref=src, dst_ref=dst, send_sem=send, recv_sem=recv, device_id=where, device_id_type=MESH
        )

    def columns(c):
        return pl.ds(pl.multiple_of(c * CHUNK, CHUNK), CHUNK)

    def scale_copy():
        return remote(scale_out, scale_in, y_send.at[chunks], y_recv.at[chunks], section=after)

    def y_copy(c):
        return remote(prev.at[:, columns(c)], rows.at[:, columns(c)], y_send.at[c], y_recv.at[c], section=after)

    def z_copy(c, k):
        node = lax.rem(n + k, experts)
        if k == 0:
            return pltpu.make_async_copy(packed.at[c, n], arrived.at[c, n, l], z_recv.at[c, 0])
        return remote(packed.at[c, node], arrived.at[c, n, l], z_send.at[c, k], z_recv.at[c, k], node=node)

    def g_copy(c, m):
        block = arrived.at[c, :, l]
        peer = sibling if m == 0 else lax.rem(l + 2 * m, members)
        return remote(block, block, g_send.at[c, m], g_recv.at[c, m], local=peer)

    def f_copy(c, m):
        block = arrived.at[c, :, lax.rem(l + members - 2 * m, members)]
        return remote(block, block, f_send.at[c, m], f_recv.at[c, m], local=sibling)

    def h_copy(k, m):
        block = hidden.at[lax.rem(n + k, experts), l]
        peer = sibling if m == 0 else lax.rem(l + 2 * m, members)
        return remote(block, block, h_send.at[k, m], h_recv.at[k, m], local=peer)

    def k_copy(k, m):
        block = hidden.at[lax.rem(n + k, experts), lax.rem(l + members - 2 * m, members)]
        return remote(block, block, k_send.at[k, m], k_recv.at[k, m], local=sibling)

    def r_copy(k, m):
        node, local = lax.rem(n + k, experts), lax.rem(l + m, members)
        if k == 0 and m == 0:
            return pltpu.make_async_copy(results.at[n, l], returned.at[n, l], r_recv.at[0, 0])
        return remote(
            results.at[node, local], returned.at[n, l], r_send.at[k, m], r_recv.at[k, m], node=node, local=local
        )

    scale_copy().start()

    @pl.loop(0, chunks)
    def _(c):
        y_copy(c).start()

    scale_copy().wait_recv()

    @pl.loop(0, chunks + 3)
    def _(step):
        @pl.when(step < chunks)
        def _():
            c = step
            y_copy(c).wait_recv()
            normed = (rows[:, columns(c)].astype(jnp.float32) * scale_in[:, 0:1] * gain[:, columns(c)]).astype(jnp.bfloat16)
            placed = jnp.dot(sel[0 : experts * slots, :], normed, preferred_element_type=jnp.float32)
            for e in range(experts):
                for half in range(HALVES):
                    packed[c, e, half * slots : (half + 1) * slots, :] = placed[
                        e * slots : (e + 1) * slots, half * part : (half + 1) * part
                    ].astype(jnp.bfloat16)
            for k in order:
                z_copy(c, k).start()

        @pl.when(jnp.logical_and(step >= 1, step < chunks + 1))
        def _():
            c = step - 1
            z_copy(c, 0).wait()
            for k in range(1, experts):
                z_copy(c, k).wait_recv()
            for m in list(range(1, chips)) + [0]:
                g_copy(c, m).start()

        @pl.when(jnp.logical_and(step >= 2, step < chunks + 2))
        def _():
            c = step - 2
            for m in range(1, chips):
                g_copy(c, m).wait_recv()
                f_copy(c, m).start()

        @pl.when(step >= 3)
        def _():
            c = step - 3

            @pl.when(c == 0)
            def _():
                for load in loads:
                    load.wait()

            g_copy(c, 0).wait_recv()
            for m in range(1, chips):
                f_copy(c, m).wait_recv()
            sides = [
                arrived[c, :, :, half * slots : (half + 1) * slots, :]
                .astype(jnp.float32).reshape(experts * group, part).astype(jnp.bfloat16)
                for half in range(HALVES)
            ]
            total[...] += jnp.dot(
                jnp.concatenate(sides, axis=1), w_in[columns(c), :], preferred_element_type=jnp.float32
            )

    for k in order:
        node = lax.rem(n + k, experts)
        span = pl.ds(pl.multiple_of(node * group, 16), group)
        gate, upper = total[span, 0:units], total[span, units : 2 * units]
        hidden[node, l] = (gate / (1.0 + jnp.exp(-gate)) * upper).astype(jnp.bfloat16)
        for m in list(range(1, chips)) + [0]:
            h_copy(k, m).start()

    for k in order:
        node = lax.rem(n + k, experts)
        for m in range(1, chips):
            h_copy(k, m).wait_recv()
            k_copy(k, m).start()
        h_copy(k, 0).wait_recv()
        for m in range(1, chips):
            k_copy(k, m).wait_recv()
        inner = jnp.concatenate([hidden[node, j] for j in range(members)], axis=1)
        made = jnp.dot(inner, w_out[...], preferred_element_type=jnp.float32)
        for j in range(members):
            for t in range(tiles):
                results[node, j, t * slots : (t + 1) * slots, 0 : ends[t]] = made[
                    j * slots : (j + 1) * slots, t * 128 : t * 128 + ends[t]
                ].astype(jnp.bfloat16)
        for m in range(members):
            r_copy(k, m).start()

    for k in order:
        for m in range(members):
            if k == 0 and m == 0:
                r_copy(k, m).wait()
            else:
                r_copy(k, m).wait_recv()

    for j in range(members):
        table = jnp.concatenate(
            [
                jnp.concatenate(
                    [returned[e, j, t * slots : (t + 1) * slots, 0 : ends[t]].astype(jnp.float32) for t in range(tiles)],
                    axis=1,
                )
                for e in range(experts)
            ],
            axis=0,
        ).astype(jnp.bfloat16)
        picked = jnp.dot(sel_t[:, 0 : experts * slots], table, preferred_element_type=jnp.float32)
        span = slice(j * width, (j + 1) * width)
        out[:, span] = (rows[:, span].astype(jnp.float32) + picked * weight[...]).astype(jnp.bfloat16)

    scale_copy().wait_send()

    @pl.loop(0, chunks)
    def _(c):
        y_copy(c).wait_send()
        for k in range(1, experts):
            z_copy(c, k).wait_send()
        for m in range(chips):
            g_copy(c, m).wait_send()
        for m in range(1, chips):
            f_copy(c, m).wait_send()

    for k in range(experts):
        for m in range(chips):
            h_copy(k, m).wait_send()
        for m in range(1, chips):
            k_copy(k, m).wait_send()
        for m in range(members):
            if k or m:
                r_copy(k, m).wait_send()


def per_device(sections, experts, members, prev_rows, expert_ids, route_weight, norm_gain, gate_weight, up_weight, down_weight):
    prev = prev_rows[0]
    tokens, feature = prev.shape
    capacity = 5 * tokens * expert_ids.shape[2] // (4 * experts)
    slots = -(-capacity // 8) * 8
    units, width = gate_weight.shape[3], down_weight.shape[3]
    chunks, chips = feature // CHUNK, members // 2
    lines = -(-(-(-width // 128) * slots) // 16) * 16
    group = members * slots
    padded = -(-(experts * slots) // 128) * 128
    bf16, f32 = jnp.bfloat16, jnp.float32
    dma = pltpu.SemaphoreType.DMA
    vmem, anywhere = pl.BlockSpec(memory_space=pltpu.VMEM), pl.BlockSpec(memory_space=pl.ANY)
    mixed = pl.pallas_call(
        functools.partial(kernel, sections, experts, members, slots),
        out_shape=jax.ShapeDtypeStruct((tokens, feature), bf16),
        in_specs=[vmem] * 4 + [anywhere] * 3,
        out_specs=vmem,
        scratch_shapes=[
            pltpu.VMEM((tokens, feature), bf16),
            pltpu.VMEM((tokens, 128), f32),
            pltpu.VMEM((tokens, 128), f32),
            pltpu.VMEM((padded, tokens), bf16),
            pltpu.VMEM((tokens, padded), bf16),
            pltpu.VMEM((chunks, experts, HALVES * slots, CHUNK // HALVES), bf16),
            pltpu.VMEM((chunks, experts, members, HALVES * slots, CHUNK // HALVES), bf16),
            pltpu.VMEM((feature, 2 * units), bf16),
            pltpu.VMEM((members * units, width), bf16),
            pltpu.VMEM((experts * group, 2 * units), f32),
            pltpu.VMEM((experts, members, group, units), bf16),
            pltpu.VMEM((experts, members, lines, 128), bf16),
            pltpu.VMEM((experts, members, lines, 128), bf16),
            dma((3,)),
            dma((chunks + 1,)), dma((chunks + 1,)),
            dma((chunks, experts)), dma((chunks, experts)),
            dma((chunks, chips)), dma((chunks, chips)),
            dma((chunks, chips)), dma((chunks, chips)),
            dma((experts, chips)), dma((experts, chips)),
            dma((experts, chips)), dma((experts, chips)),
            dma((experts, members)), dma((experts, members)),
        ],
        compiler_params=pltpu.CompilerParams(
            collective_id=0, has_side_effects=True, vmem_limit_bytes=56 * 1024 * 1024
        ),
    )(prev, expert_ids[0], route_weight[0], norm_gain, gate_weight[0, 0], up_weight[0, 0], down_weight[0, 0])
    return mixed[None]


def solution(mesh):
    placed = (
        P("section", ("node", "local"), None),
        P("section", ("node", "local"), None),
        P("section", ("node", "local"), None),
        P("section", None),
        P("section", "node", None, "local"),
        P("section", "node", None, "local"),
        P("section", "node", None, "local"),
    )
    sizes = mesh.shape
    return jax.shard_map(
        functools.partial(per_device, sizes["section"], sizes["node"], sizes["local"]),
        mesh=mesh,
        in_specs=placed,
        out_specs=P("section", ("node", "local"), None),
        check_vma=False,
    )
```

```python
import functools

import jax
import jax.numpy as jnp
from jax import lax
from jax.experimental import pallas as pl
from jax.experimental.pallas import tpu as pltpu
from jax.sharding import PartitionSpec as P

MESH = pl.DeviceIdType.MESH
HALVES = 2
CHUNK = 512
LAG = 3


def split(slots):
    first = 8 * -(-slots // 16)
    return (first, slots - first)


def kernel(sections, experts, members, slots, prev, ids, weight, gain, w_gate, w_up, w_down, out, *scratch):
    rows, normal, scale_out, scale_in, scale, mid, w_in, w_out, w_sem, y_send, y_recv = scratch[:11]
    own = (len(scratch) - 11) // 2
    parts = [scratch[11 : 11 + own], scratch[11 + own :]]
    s, n, l = lax.axis_index("section"), lax.axis_index("node"), lax.axis_index("local")
    tokens, feature = prev.shape
    chunks = feature // CHUNK
    part = CHUNK // HALVES
    units = w_gate.shape[1]
    width = w_down.shape[1]
    tiles = -(-width // 128)
    ends = [min(128, width - 128 * t) for t in range(tiles)]
    chips = members // 2
    sibling = l + 1 - 2 * lax.rem(l, 2)
    order = sorted(range(experts), key=lambda k: -min(k, experts - k))

    loads = [
        pltpu.make_async_copy(w_gate, w_in.at[:, pl.ds(0, units)], w_sem.at[0]),
        pltpu.make_async_copy(w_up, w_in.at[:, pl.ds(units, units)], w_sem.at[1]),
        pltpu.make_async_copy(w_down, w_out, w_sem.at[2]),
    ]
    for load in loads:
        load.start()

    barrier = pltpu.get_barrier_semaphore()
    after, before = lax.rem(s + 1, sections), lax.rem(s + sections - 1, sections)
    for other in (after, before):
        pl.semaphore_signal(barrier, inc=1, device_id={"section": other, "node": n, "local": l}, device_id_type=MESH)
    for k in range(experts):
        for m in range(members):
            if k or m:
                place = {"section": s, "node": lax.rem(n + k, experts), "local": lax.rem(l + m, members)}
                pl.semaphore_signal(barrier, inc=1, device_id=place, device_id_type=MESH)

    wide = prev[...].astype(jnp.float32)
    mean = jnp.sum(wide * wide, axis=1, keepdims=True) / feature
    scale_out[...] = jnp.broadcast_to(lax.rsqrt(mean + 1e-06), (tokens, 128)).T[0:8, :]

    chosen = jnp.broadcast_to(ids[...].astype(jnp.float32), (128, tokens)).T
    lanes = lax.broadcasted_iota(jnp.int32, (tokens, 128), 1).astype(jnp.float32)
    onehot = jnp.where(chosen == lanes, 1.0, 0.0)
    earlier = lax.broadcasted_iota(jnp.int32, (tokens, tokens), 1) < lax.broadcasted_iota(jnp.int32, (tokens, tokens), 0)
    counts = jnp.dot(
        jnp.where(earlier, 1.0, 0.0).astype(jnp.bfloat16), onehot.astype(jnp.bfloat16),
        preferred_element_type=jnp.float32,
    )
    slot = jnp.sum(counts * onehot, axis=1, keepdims=True)
    pool = split(slots)
    for p in range(2):
        sel, sel_t, total = parts[p][0], parts[p][1], parts[p][4]
        local_slot = slot - (pool[0] if p else 0)
        inside = jnp.logical_and(local_slot >= 0, local_slot < pool[p])
        target = jnp.where(inside, chosen[:, 0:1] * pool[p] + local_slot, -1.0)
        places = lax.broadcasted_iota(jnp.int32, (tokens, sel.shape[0]), 1).astype(jnp.float32)
        spread = jnp.where(target == places, 1.0, 0.0)
        sel_t[...] = spread.astype(jnp.bfloat16)
        sel[...] = spread.T.astype(jnp.bfloat16)
        total[...] = jnp.zeros_like(total)
    factor = jnp.broadcast_to(weight[...], (128, tokens)).T[:, 0:1]

    pl.semaphore_wait(barrier, experts * members + 1)

    def remote(src, dst, send, recv, **place):
        where = {"section": s, "node": n, "local": l}
        where.update(place)
        return pltpu.make_async_remote_copy(
            src_ref=src, dst_ref=dst, send_sem=send, recv_sem=recv, device_id=where, device_id_type=MESH
        )

    def columns(c):
        return pl.ds(pl.multiple_of(c * CHUNK, CHUNK), CHUNK)

    def scale_copy():
        return remote(scale_out, scale_in, y_send.at[chunks], y_recv.at[chunks], section=after)

    def y_copy(c):
        return remote(prev.at[:, columns(c)], rows.at[:, columns(c)], y_send.at[c], y_recv.at[c], section=after)

    class Part:
        def __init__(self, p):
            self.p, self.slots, self.group = p, pool[p], members * pool[p]
            (self.sel, self.sel_t, self.packed, self.arrived, self.total, self.hidden, self.results, self.returned,
             self.z_send, self.z_recv, self.g_send, self.g_recv, self.f_send, self.f_recv,
             self.h_send, self.h_recv, self.k_send, self.k_recv, self.r_send, self.r_recv) = parts[p]

        def z_copy(self, c, k):
            node = lax.rem(n + k, experts)
            if k == 0:
                return pltpu.make_async_copy(self.packed.at[c, n], self.arrived.at[c, n, l], self.z_recv.at[c, 0])
            return remote(
                self.packed.at[c, node], self.arrived.at[c, n, l], self.z_send.at[c, k], self.z_recv.at[c, k], node=node
            )

        def g_copy(self, c, m):
            block = self.arrived.at[c, :, l]
            peer = sibling if m == 0 else lax.rem(l + 2 * m, members)
            return remote(block, block, self.g_send.at[c, m], self.g_recv.at[c, m], local=peer)

        def f_copy(self, c, m):
            block = self.arrived.at[c, :, lax.rem(l + members - 2 * m, members)]
            return remote(block, block, self.f_send.at[c, m], self.f_recv.at[c, m], local=sibling)

        def h_copy(self, k, m):
            block = self.hidden.at[lax.rem(n + k, experts), l]
            peer = sibling if m == 0 else lax.rem(l + 2 * m, members)
            return remote(block, block, self.h_send.at[k, m], self.h_recv.at[k, m], local=peer)

        def k_copy(self, k, m):
            block = self.hidden.at[lax.rem(n + k, experts), lax.rem(l + members - 2 * m, members)]
            return remote(block, block, self.k_send.at[k, m], self.k_recv.at[k, m], local=sibling)

        def r_copy(self, k, m):
            node, local = lax.rem(n + k, experts), lax.rem(l + m, members)
            if k == 0 and m == 0:
                return pltpu.make_async_copy(self.results.at[n, l], self.returned.at[n, l], self.r_recv.at[0, 0])
            return remote(
                self.results.at[node, local], self.returned.at[n, l], self.r_send.at[k, m], self.r_recv.at[k, m],
                node=node, local=local,
            )

        def dispatch(self, c):
            if self.p == 0:
                y_copy(c).wait_recv()
                normed = (
                    rows[:, columns(c)].astype(jnp.float32) * scale[:, 0:1] * gain[:, columns(c)]
                ).astype(jnp.bfloat16)
                normal[:, columns(c)] = normed
            else:
                normed = normal[:, columns(c)]
            placed = jnp.dot(
                self.sel[0 : experts * self.slots, :], normed, preferred_element_type=jnp.float32
            )
            for e in range(experts):
                for half in range(HALVES):
                    self.packed[c, e, half * self.slots : (half + 1) * self.slots, :] = placed[
                        e * self.slots : (e + 1) * self.slots, half * part : (half + 1) * part
                    ].astype(jnp.bfloat16)
            for k in order:
                self.z_copy(c, k).start()

        def share(self, c):
            self.z_copy(c, 0).wait()
            for k in range(1, experts):
                self.z_copy(c, k).wait_recv()
            for m in list(range(1, chips)) + [0]:
                self.g_copy(c, m).start()

        def hand_on(self, c):
            for m in range(1, chips):
                self.g_copy(c, m).wait_recv()
                self.f_copy(c, m).start()

        def multiply(self, c):
            self.g_copy(c, 0).wait_recv()
            for m in range(1, chips):
                self.f_copy(c, m).wait_recv()
            sides = [
                self.arrived[c, :, :, half * self.slots : (half + 1) * self.slots, :]
                .astype(jnp.float32).reshape(experts * self.group, part).astype(jnp.bfloat16)
                for half in range(HALVES)
            ]
            self.total[...] += jnp.dot(
                jnp.concatenate(sides, axis=1), w_in[columns(c), :], preferred_element_type=jnp.float32
            )

        def activate(self):
            for k in order:
                node = lax.rem(n + k, experts)
                span = pl.ds(pl.multiple_of(node * self.group, 16), self.group)
                gate, upper = self.total[span, 0:units], self.total[span, units : 2 * units]
                self.hidden[node, l] = (gate / (1.0 + jnp.exp(-gate)) * upper).astype(jnp.bfloat16)
                for m in list(range(1, chips)) + [0]:
                    self.h_copy(k, m).start()

        def give_back(self):
            for k in order:
                node = lax.rem(n + k, experts)
                for m in range(1, chips):
                    self.h_copy(k, m).wait_recv()
                    self.k_copy(k, m).start()
                self.h_copy(k, 0).wait_recv()
                for m in range(1, chips):
                    self.k_copy(k, m).wait_recv()
                inner = jnp.concatenate([self.hidden[node, j] for j in range(members)], axis=1)
                made = jnp.dot(inner, w_out[...], preferred_element_type=jnp.float32)
                for j in range(members):
                    for t in range(tiles):
                        self.results[node, j, t * self.slots : (t + 1) * self.slots, 0 : ends[t]] = made[
                            j * self.slots : (j + 1) * self.slots, t * 128 : t * 128 + ends[t]
                        ].astype(jnp.bfloat16)
                for m in range(members):
                    self.r_copy(k, m).start()

        def collect(self):
            for k in order:
                for m in range(members):
                    if k == 0 and m == 0:
                        self.r_copy(k, m).wait()
                    else:
                        self.r_copy(k, m).wait_recv()

        def picked(self, j):
            table = jnp.concatenate(
                [
                    jnp.concatenate(
                        [
                            self.returned[e, j, t * self.slots : (t + 1) * self.slots, 0 : ends[t]].astype(jnp.float32)
                            for t in range(tiles)
                        ],
                        axis=1,
                    )
                    for e in range(experts)
                ],
                axis=0,
            ).astype(jnp.bfloat16)
            return jnp.dot(self.sel_t[:, 0 : experts * self.slots], table, preferred_element_type=jnp.float32)

        def settle(self):
            @pl.loop(0, chunks)
            def _(c):
                for k in range(1, experts):
                    self.z_copy(c, k).wait_send()
                for m in range(chips):
                    self.g_copy(c, m).wait_send()
                for m in range(1, chips):
                    self.f_copy(c, m).wait_send()

            for k in range(experts):
                for m in range(chips):
                    self.h_copy(k, m).wait_send()
                for m in range(1, chips):
                    self.k_copy(k, m).wait_send()
                for m in range(members):
                    if k or m:
                        self.r_copy(k, m).wait_send()

    first, second = Part(0), Part(1)
    scale_copy().start()

    @pl.loop(0, chunks)
    def _(c):
        y_copy(c).start()

    scale_copy().wait_recv()
    scale[...] = jnp.broadcast_to(scale_in[0:1, :], (128, tokens)).T

    @pl.loop(0, chunks)
    def _(step):
        first.dispatch(step)

        def at(lag, stage):
            @pl.when(step >= lag)
            def _():
                stage(step - lag)

        at(LAG, second.dispatch)
        at(1, first.share)
        at(2, first.hand_on)

        @pl.when(step == 3)
        def _():
            for load in loads:
                load.wait()

        at(3, first.multiply)
        at(LAG + 1, second.share)
        at(LAG + 2, second.hand_on)
        at(LAG + 3, second.multiply)

    first.share(chunks - 1)
    pl.loop(chunks - LAG, chunks)(second.dispatch)
    first.hand_on(chunks - 2)
    first.multiply(chunks - 3)
    first.hand_on(chunks - 1)
    pl.loop(chunks - 2, chunks)(first.multiply)
    first.activate()
    pl.loop(chunks - LAG - 1, chunks - 1)(second.share)
    first.give_back()
    pl.loop(chunks - LAG - 2, chunks - 1)(second.hand_on)
    second.share(chunks - 1)
    pl.loop(chunks - LAG - 3, chunks - 1)(second.multiply)
    second.hand_on(chunks - 1)
    second.multiply(chunks - 1)
    second.activate()
    second.give_back()
    first.collect()
    for j in range(members):
        span = slice(j * width, (j + 1) * width)
        mid[:, span] = rows[:, span].astype(jnp.float32) + first.picked(j) * factor
    second.collect()
    for j in range(members):
        span = slice(j * width, (j + 1) * width)
        out[:, span] = (mid[:, span] + second.picked(j) * factor).astype(jnp.bfloat16)

    scale_copy().wait_send()

    @pl.loop(0, chunks)
    def _(c):
        y_copy(c).wait_send()

    first.settle()
    second.settle()


def per_device(sections, experts, members, prev_rows, expert_ids, route_weight, norm_gain, gate_weight, up_weight, down_weight):
    prev = prev_rows[0]
    tokens, feature = prev.shape
    capacity = 5 * tokens * expert_ids.shape[2] // (4 * experts)
    slots = -(-capacity // 8) * 8
    units, width = gate_weight.shape[3], down_weight.shape[3]
    chunks, chips = feature // CHUNK, members // 2
    bf16, f32 = jnp.bfloat16, jnp.float32
    dma = pltpu.SemaphoreType.DMA
    vmem, anywhere = pl.BlockSpec(memory_space=pltpu.VMEM), pl.BlockSpec(memory_space=pl.ANY)
    scratch = [
        pltpu.VMEM((tokens, feature), bf16),
        pltpu.VMEM((tokens, feature), bf16),
        pltpu.VMEM((8, tokens), f32),
        pltpu.VMEM((8, tokens), f32),
        pltpu.VMEM((tokens, 128), f32),
        pltpu.VMEM((tokens, feature), f32),
        pltpu.VMEM((feature, 2 * units), bf16),
        pltpu.VMEM((members * units, width), bf16),
        dma((3,)),
        dma((chunks + 1,)), dma((chunks + 1,)),
    ]
    for some in split(slots):
        lines = -(-(-(-width // 128) * some) // 16) * 16
        group = members * some
        padded = -(-(experts * some) // 128) * 128
        scratch += [
            pltpu.VMEM((padded, tokens), bf16),
            pltpu.VMEM((tokens, padded), bf16),
            pltpu.VMEM((chunks, experts, HALVES * some, CHUNK // HALVES), bf16),
            pltpu.VMEM((chunks, experts, members, HALVES * some, CHUNK // HALVES), bf16),
            pltpu.VMEM((experts * group, 2 * units), f32),
            pltpu.VMEM((experts, members, group, units), bf16),
            pltpu.VMEM((experts, members, lines, 128), bf16),
            pltpu.VMEM((experts, members, lines, 128), bf16),
            dma((chunks, experts)), dma((chunks, experts)),
            dma((chunks, chips)), dma((chunks, chips)),
            dma((chunks, chips)), dma((chunks, chips)),
            dma((experts, chips)), dma((experts, chips)),
            dma((experts, chips)), dma((experts, chips)),
            dma((experts, members)), dma((experts, members)),
        ]
    mixed = pl.pallas_call(
        functools.partial(kernel, sections, experts, members, slots),
        out_shape=jax.ShapeDtypeStruct((tokens, feature), bf16),
        in_specs=[vmem] * 4 + [anywhere] * 3,
        out_specs=vmem,
        scratch_shapes=scratch,
        compiler_params=pltpu.CompilerParams(
            collective_id=0, has_side_effects=True, vmem_limit_bytes=56 * 1024 * 1024
        ),
    )(
        prev, expert_ids[0].reshape(1, tokens), route_weight[0].reshape(1, tokens), norm_gain,
        gate_weight[0, 0], up_weight[0, 0], down_weight[0, 0],
    )
    return mixed[None]


def solution(mesh):
    placed = (
        P("section", ("node", "local"), None),
        P("section", ("node", "local"), None),
        P("section", ("node", "local"), None),
        P("section", None),
        P("section", "node", None, "local"),
        P("section", "node", None, "local"),
        P("section", "node", None, "local"),
    )
    sizes = mesh.shape
    return jax.shard_map(
        functools.partial(per_device, sizes["section"], sizes["node"], sizes["local"]),
        mesh=mesh,
        in_specs=placed,
        out_specs=P("section", ("node", "local"), None),
        check_vma=False,
    )
```

```python
import functools

import jax
import jax.numpy as jnp
from jax import lax
from jax.experimental import pallas as pl
from jax.experimental.pallas import tpu as pltpu
from jax.sharding import PartitionSpec as P

MESH = pl.DeviceIdType.MESH
HALVES = 2
CHUNK = 512
LAG = 4
AHEAD = 3


def split(slots):
    first = 8 * -(-slots // 16)
    return (first, slots - first)


def kernel(sections, experts, members, slots, prev, ids, weight, gain, w_gate, w_up, w_down, out, *scratch):
    rows, normal, scale_out, scale_in, scale, mid, w_in, w_out, w_sem, y_send, y_recv = scratch[:11]
    own = (len(scratch) - 11) // 2
    parts = [scratch[11 : 11 + own], scratch[11 + own :]]
    s, n, l = lax.axis_index("section"), lax.axis_index("node"), lax.axis_index("local")
    tokens, feature = prev.shape
    chunks = feature // CHUNK
    part = CHUNK // HALVES
    units = w_gate.shape[1]
    width = w_down.shape[1]
    tiles = -(-width // 128)
    ends = [min(128, width - 128 * t) for t in range(tiles)]
    chips = members // 2
    sibling = l + 1 - 2 * lax.rem(l, 2)
    order = sorted(range(experts), key=lambda k: -min(k, experts - k))

    loads = [
        pltpu.make_async_copy(w_gate, w_in.at[:, pl.ds(0, units)], w_sem.at[0]),
        pltpu.make_async_copy(w_up, w_in.at[:, pl.ds(units, units)], w_sem.at[1]),
        pltpu.make_async_copy(w_down, w_out, w_sem.at[2]),
    ]
    for load in loads:
        load.start()

    barrier = pltpu.get_barrier_semaphore()
    after, before = lax.rem(s + 1, sections), lax.rem(s + sections - 1, sections)
    for other in (after, before):
        pl.semaphore_signal(barrier, inc=1, device_id={"section": other, "node": n, "local": l}, device_id_type=MESH)
    for k in range(experts):
        for m in range(members):
            if k or m:
                place = {"section": s, "node": lax.rem(n + k, experts), "local": lax.rem(l + m, members)}
                pl.semaphore_signal(barrier, inc=1, device_id=place, device_id_type=MESH)

    wide = prev[...].astype(jnp.float32)
    mean = jnp.sum(wide * wide, axis=1, keepdims=True) / feature
    scale_out[...] = jnp.broadcast_to(lax.rsqrt(mean + 1e-06), (tokens, 128)).T[0:8, :]

    chosen = jnp.broadcast_to(ids[...].astype(jnp.float32), (128, tokens)).T
    lanes = lax.broadcasted_iota(jnp.int32, (tokens, 128), 1).astype(jnp.float32)
    onehot = jnp.where(chosen == lanes, 1.0, 0.0)
    earlier = lax.broadcasted_iota(jnp.int32, (tokens, tokens), 1) < lax.broadcasted_iota(jnp.int32, (tokens, tokens), 0)
    counts = jnp.dot(
        jnp.where(earlier, 1.0, 0.0).astype(jnp.bfloat16), onehot.astype(jnp.bfloat16),
        preferred_element_type=jnp.float32,
    )
    slot = jnp.sum(counts * onehot, axis=1, keepdims=True)
    pool = split(slots)
    for p in range(2):
        sel, sel_t, total = parts[p][0], parts[p][1], parts[p][4]
        local_slot = slot - (pool[0] if p else 0)
        inside = jnp.logical_and(local_slot >= 0, local_slot < pool[p])
        target = jnp.where(inside, chosen[:, 0:1] * pool[p] + local_slot, -1.0)
        places = lax.broadcasted_iota(jnp.int32, (tokens, sel.shape[0]), 1).astype(jnp.float32)
        spread = jnp.where(target == places, 1.0, 0.0)
        sel_t[...] = spread.astype(jnp.bfloat16)
        sel[...] = spread.T.astype(jnp.bfloat16)
        total[...] = jnp.zeros_like(total)
    factor = jnp.broadcast_to(weight[...], (128, tokens)).T[:, 0:1]

    pl.semaphore_wait(barrier, experts * members + 1)

    def remote(src, dst, send, recv, **place):
        where = {"section": s, "node": n, "local": l}
        where.update(place)
        return pltpu.make_async_remote_copy(
            src_ref=src, dst_ref=dst, send_sem=send, recv_sem=recv, device_id=where, device_id_type=MESH
        )

    def columns(c):
        return pl.ds(pl.multiple_of(c * CHUNK, CHUNK), CHUNK)

    def scale_copy():
        return remote(scale_out, scale_in, y_send.at[chunks], y_recv.at[chunks], section=after)

    def y_copy(c):
        return remote(prev.at[:, columns(c)], rows.at[:, columns(c)], y_send.at[c], y_recv.at[c], section=after)

    class Part:
        def __init__(self, p):
            self.p, self.slots, self.group = p, pool[p], members * pool[p]
            (self.sel, self.sel_t, self.packed, self.arrived, self.total, self.hidden, self.results, self.returned,
             self.z_send, self.z_recv, self.g_send, self.g_recv, self.f_send, self.f_recv,
             self.h_send, self.h_recv, self.k_send, self.k_recv, self.r_send, self.r_recv) = parts[p]

        def z_copy(self, c, k):
            node = lax.rem(n + k, experts)
            if k == 0:
                return pltpu.make_async_copy(self.packed.at[c, n], self.arrived.at[c, n, l], self.z_recv.at[c, 0])
            return remote(
                self.packed.at[c, node], self.arrived.at[c, n, l], self.z_send.at[c, k], self.z_recv.at[c, k], node=node
            )

        def g_copy(self, c, m):
            block = self.arrived.at[c, :, l]
            peer = sibling if m == 0 else lax.rem(l + 2 * m, members)
            return remote(block, block, self.g_send.at[c, m], self.g_recv.at[c, m], local=peer)

        def f_copy(self, c, m):
            block = self.arrived.at[c, :, lax.rem(l + members - 2 * m, members)]
            return remote(block, block, self.f_send.at[c, m], self.f_recv.at[c, m], local=sibling)

        def h_copy(self, k, m):
            block = self.hidden.at[lax.rem(n + k, experts), l]
            peer = sibling if m == 0 else lax.rem(l + 2 * m, members)
            return remote(block, block, self.h_send.at[k, m], self.h_recv.at[k, m], local=peer)

        def k_copy(self, k, m):
            block = self.hidden.at[lax.rem(n + k, experts), lax.rem(l + members - 2 * m, members)]
            return remote(block, block, self.k_send.at[k, m], self.k_recv.at[k, m], local=sibling)

        def r_copy(self, k, m):
            node, local = lax.rem(n + k, experts), lax.rem(l + m, members)
            if k == 0 and m == 0:
                return pltpu.make_async_copy(self.results.at[n, l], self.returned.at[n, l], self.r_recv.at[0, 0])
            return remote(
                self.results.at[node, local], self.returned.at[n, l], self.r_send.at[k, m], self.r_recv.at[k, m],
                node=node, local=local,
            )

        def dispatch(self, c):
            if self.p == 0:
                normed = (
                    rows[:, columns(c)].astype(jnp.float32) * scale[:, 0:1] * gain[:, columns(c)]
                ).astype(jnp.bfloat16)
                normal[:, columns(c)] = normed
            else:
                normed = normal[:, columns(c)]
            placed = jnp.dot(
                self.sel[0 : experts * self.slots, :], normed, preferred_element_type=jnp.float32
            )
            for e in range(experts):
                for half in range(HALVES):
                    self.packed[c, e, half * self.slots : (half + 1) * self.slots, :] = placed[
                        e * self.slots : (e + 1) * self.slots, half * part : (half + 1) * part
                    ].astype(jnp.bfloat16)
            for k in order:
                self.z_copy(c, k).start()

        def share(self, c):
            self.z_copy(c, 0).wait()
            for k in range(1, experts):
                self.z_copy(c, k).wait_recv()
            for m in list(range(1, chips)) + [0]:
                self.g_copy(c, m).start()

        def hand_on(self, c):
            for m in range(1, chips):
                self.g_copy(c, m).wait_recv()
                self.f_copy(c, m).start()

        def multiply(self, c):
            self.g_copy(c, 0).wait_recv()
            for m in range(1, chips):
                self.f_copy(c, m).wait_recv()
            sides = [
                self.arrived[c, :, :, half * self.slots : (half + 1) * self.slots, :]
                .astype(jnp.float32).reshape(experts * self.group, part).astype(jnp.bfloat16)
                for half in range(HALVES)
            ]
            self.total[...] += jnp.dot(
                jnp.concatenate(sides, axis=1), w_in[columns(c), :], preferred_element_type=jnp.float32
            )

        def activate(self):
            for k in order:
                node = lax.rem(n + k, experts)
                span = pl.ds(pl.multiple_of(node * self.group, 16), self.group)
                gate, upper = self.total[span, 0:units], self.total[span, units : 2 * units]
                self.hidden[node, l] = (gate / (1.0 + jnp.exp(-gate)) * upper).astype(jnp.bfloat16)
                for m in list(range(1, chips)) + [0]:
                    self.h_copy(k, m).start()

        def pass_hidden(self, k):
            for m in range(1, chips):
                self.h_copy(k, m).wait_recv()
                self.k_copy(k, m).start()

        def give_back(self):
            self.pass_hidden(order[0])
            for i, k in enumerate(order):
                node = lax.rem(n + k, experts)
                if i + 1 < experts:
                    self.pass_hidden(order[i + 1])
                self.h_copy(k, 0).wait_recv()
                for m in range(1, chips):
                    self.k_copy(k, m).wait_recv()
                inner = jnp.concatenate([self.hidden[node, j] for j in range(members)], axis=1)
                made = jnp.dot(inner, w_out[...], preferred_element_type=jnp.float32)
                for j in range(members):
                    for t in range(tiles):
                        self.results[node, j, t * self.slots : (t + 1) * self.slots, 0 : ends[t]] = made[
                            j * self.slots : (j + 1) * self.slots, t * 128 : t * 128 + ends[t]
                        ].astype(jnp.bfloat16)
                for m in range(members):
                    self.r_copy(k, m).start()

        def collect(self):
            for k in order:
                for m in range(members):
                    if k == 0 and m == 0:
                        self.r_copy(k, m).wait()
                    else:
                        self.r_copy(k, m).wait_recv()

        def picked(self, j):
            table = jnp.concatenate(
                [
                    jnp.concatenate(
                        [
                            self.returned[e, j, t * self.slots : (t + 1) * self.slots, 0 : ends[t]].astype(jnp.float32)
                            for t in range(tiles)
                        ],
                        axis=1,
                    )
                    for e in range(experts)
                ],
                axis=0,
            ).astype(jnp.bfloat16)
            return jnp.dot(self.sel_t[:, 0 : experts * self.slots], table, preferred_element_type=jnp.float32)

        def settle(self):
            @pl.loop(0, chunks)
            def _(c):
                for k in range(1, experts):
                    self.z_copy(c, k).wait_send()
                for m in range(chips):
                    self.g_copy(c, m).wait_send()
                for m in range(1, chips):
                    self.f_copy(c, m).wait_send()

            for k in range(experts):
                for m in range(chips):
                    self.h_copy(k, m).wait_send()
                for m in range(1, chips):
                    self.k_copy(k, m).wait_send()
                for m in range(members):
                    if k or m:
                        self.r_copy(k, m).wait_send()

    first, second = Part(0), Part(1)
    scale_copy().start()

    for c in range(AHEAD):
        y_copy(c).start()

    scale_copy().wait_recv()
    scale[...] = jnp.broadcast_to(scale_in[0:1, :], (128, tokens)).T

    @pl.loop(0, chunks)
    def _(step):
        y_copy(step).wait_recv()

        @pl.when(step + AHEAD < chunks)
        def _():
            y_copy(step + AHEAD).start()

        first.dispatch(step)

        def at(lag, stage):
            @pl.when(step >= lag)
            def _():
                stage(step - lag)

        at(LAG, second.dispatch)
        at(2, first.share)
        at(4, first.hand_on)

        @pl.when(step == 5)
        def _():
            for load in loads:
                load.wait()

        at(5, first.multiply)
        at(LAG + 2, second.share)

    pl.loop(chunks - LAG, chunks - 2)(second.dispatch)
    first.share(chunks - 2)
    pl.loop(chunks - 2, chunks)(second.dispatch)
    first.hand_on(chunks - 4)
    first.multiply(chunks - 5)
    first.hand_on(chunks - 3)
    first.multiply(chunks - 4)
    first.share(chunks - 1)
    first.hand_on(chunks - 2)
    pl.loop(chunks - 3, chunks - 1)(first.multiply)
    first.hand_on(chunks - 1)
    first.multiply(chunks - 1)
    first.activate()
    pl.loop(chunks - LAG - 2, chunks - 1)(second.share)
    first.give_back()
    second.share(chunks - 1)
    pl.loop(0, chunks - 1)(second.hand_on)
    pl.loop(0, chunks - 1)(second.multiply)
    second.hand_on(chunks - 1)
    second.multiply(chunks - 1)
    second.activate()
    second.give_back()
    first.collect()
    for j in range(members):
        span = slice(j * width, (j + 1) * width)
        mid[:, span] = rows[:, span].astype(jnp.float32) + first.picked(j) * factor
    second.collect()
    for j in range(members):
        span = slice(j * width, (j + 1) * width)
        out[:, span] = (mid[:, span] + second.picked(j) * factor).astype(jnp.bfloat16)

    scale_copy().wait_send()

    @pl.loop(0, chunks)
    def _(c):
        y_copy(c).wait_send()

    first.settle()
    second.settle()


def per_device(sections, experts, members, prev_rows, expert_ids, route_weight, norm_gain, gate_weight, up_weight, down_weight):
    prev = prev_rows[0]
    tokens, feature = prev.shape
    capacity = 5 * tokens * expert_ids.shape[2] // (4 * experts)
    slots = -(-capacity // 8) * 8
    units, width = gate_weight.shape[3], down_weight.shape[3]
    chunks, chips = feature // CHUNK, members // 2
    bf16, f32 = jnp.bfloat16, jnp.float32
    dma = pltpu.SemaphoreType.DMA
    vmem, anywhere = pl.BlockSpec(memory_space=pltpu.VMEM), pl.BlockSpec(memory_space=pl.ANY)
    scratch = [
        pltpu.VMEM((tokens, feature), bf16),
        pltpu.VMEM((tokens, feature), bf16),
        pltpu.VMEM((8, tokens), f32),
        pltpu.VMEM((8, tokens), f32),
        pltpu.VMEM((tokens, 128), f32),
        pltpu.VMEM((tokens, feature), f32),
        pltpu.VMEM((feature, 2 * units), bf16),
        pltpu.VMEM((members * units, width), bf16),
        dma((3,)),
        dma((chunks + 1,)), dma((chunks + 1,)),
    ]
    for some in split(slots):
        lines = -(-(-(-width // 128) * some) // 16) * 16
        group = members * some
        padded = -(-(experts * some) // 128) * 128
        scratch += [
            pltpu.VMEM((padded, tokens), bf16),
            pltpu.VMEM((tokens, padded), bf16),
            pltpu.VMEM((chunks, experts, HALVES * some, CHUNK // HALVES), bf16),
            pltpu.VMEM((chunks, experts, members, HALVES * some, CHUNK // HALVES), bf16),
            pltpu.VMEM((experts * group, 2 * units), f32),
            pltpu.VMEM((experts, members, group, units), bf16),
            pltpu.VMEM((experts, members, lines, 128), bf16),
            pltpu.VMEM((experts, members, lines, 128), bf16),
            dma((chunks, experts)), dma((chunks, experts)),
            dma((chunks, chips)), dma((chunks, chips)),
            dma((chunks, chips)), dma((chunks, chips)),
            dma((experts, chips)), dma((experts, chips)),
            dma((experts, chips)), dma((experts, chips)),
            dma((experts, members)), dma((experts, members)),
        ]
    mixed = pl.pallas_call(
        functools.partial(kernel, sections, experts, members, slots),
        out_shape=jax.ShapeDtypeStruct((tokens, feature), bf16),
        in_specs=[vmem] * 4 + [anywhere] * 3,
        out_specs=vmem,
        scratch_shapes=scratch,
        compiler_params=pltpu.CompilerParams(
            collective_id=0, has_side_effects=True, vmem_limit_bytes=56 * 1024 * 1024
        ),
    )(
        prev, expert_ids[0].reshape(1, tokens), route_weight[0].reshape(1, tokens), norm_gain,
        gate_weight[0, 0], up_weight[0, 0], down_weight[0, 0],
    )
    return mixed[None]


def solution(mesh):
    placed = (
        P("section", ("node", "local"), None),
        P("section", ("node", "local"), None),
        P("section", ("node", "local"), None),
        P("section", None),
        P("section", "node", None, "local"),
        P("section", "node", None, "local"),
        P("section", "node", None, "local"),
    )
    sizes = mesh.shape
    return jax.shard_map(
        functools.partial(per_device, sizes["section"], sizes["node"], sizes["local"]),
        mesh=mesh,
        in_specs=placed,
        out_specs=P("section", ("node", "local"), None),
        check_vma=False,
    )
```

```python
import functools

import jax
import jax.numpy as jnp
from jax import lax
from jax.experimental import pallas as pl
from jax.experimental.pallas import tpu as pltpu
from jax.sharding import PartitionSpec as P

MESH = pl.DeviceIdType.MESH
HALVES = 2
CHUNK = 512


def split(slots):
    first = 8 * -(-slots // 16)
    return (first, slots - first)


def kernel(sections, experts, members, slots, prev, ids, weight, gain, w_gate, w_up, w_down, out, *scratch):
    rows, normal, ids_in, gain_in, mid, w_in, w_out, w_sem, y_send, y_recv = scratch[:10]
    own = (len(scratch) - 10) // 2
    parts = [scratch[10 : 10 + own], scratch[10 + own :]]
    s, n, l = lax.axis_index("section"), lax.axis_index("node"), lax.axis_index("local")
    tokens, feature = prev.shape
    chunks = feature // CHUNK
    part = CHUNK // HALVES
    units = w_gate.shape[1]
    width = w_down.shape[1]
    tiles = -(-width // 128)
    ends = [min(128, width - 128 * t) for t in range(tiles)]
    chips = members // 2
    sibling = l + 1 - 2 * lax.rem(l, 2)
    order = sorted(range(experts), key=lambda k: -min(k, experts - k))

    loads = [
        pltpu.make_async_copy(w_gate, w_in.at[:, pl.ds(0, units)], w_sem.at[0]),
        pltpu.make_async_copy(w_up, w_in.at[:, pl.ds(units, units)], w_sem.at[1]),
        pltpu.make_async_copy(w_down, w_out, w_sem.at[2]),
    ]
    for load in loads:
        load.start()

    barrier = pltpu.get_barrier_semaphore()
    after, before = lax.rem(s + 1, sections), lax.rem(s + sections - 1, sections)
    pl.semaphore_signal(barrier, inc=1, device_id={"section": after, "node": n, "local": l}, device_id_type=MESH)
    for k in range(experts):
        node = lax.rem(n + k, experts)
        pl.semaphore_signal(barrier, inc=1, device_id={"section": before, "node": node, "local": l}, device_id_type=MESH)
        for m in range(members):
            if k or m:
                place = {"section": s, "node": node, "local": lax.rem(l + m, members)}
                pl.semaphore_signal(barrier, inc=1, device_id=place, device_id_type=MESH)

    pool = split(slots)

    def spreads(row):
        chosen = jnp.broadcast_to(row.astype(jnp.float32), (128, tokens)).T
        lanes = lax.broadcasted_iota(jnp.int32, (tokens, 128), 1).astype(jnp.float32)
        onehot = jnp.where(chosen == lanes, 1.0, 0.0)
        earlier = lax.broadcasted_iota(jnp.int32, (tokens, tokens), 1) < lax.broadcasted_iota(
            jnp.int32, (tokens, tokens), 0
        )
        counts = jnp.dot(
            jnp.where(earlier, 1.0, 0.0).astype(jnp.bfloat16), onehot.astype(jnp.bfloat16),
            preferred_element_type=jnp.float32,
        )
        slot = jnp.sum(counts * onehot, axis=1, keepdims=True)
        made = []
        for p in range(2):
            local_slot = slot - (pool[0] if p else 0)
            inside = jnp.logical_and(local_slot >= 0, local_slot < pool[p])
            target = jnp.where(inside, chosen[:, 0:1] * pool[p] + local_slot, -1.0)
            places = lax.broadcasted_iota(jnp.int32, (tokens, parts[p][0].shape[0]), 1).astype(jnp.float32)
            made.append(jnp.where(target == places, 1.0, 0.0))
        return made

    for p, spread in enumerate(spreads(ids[...])):
        parts[p][1][...] = spread.astype(jnp.bfloat16)
        parts[p][4][...] = jnp.zeros_like(parts[p][4])
    wide = prev[...].astype(jnp.float32)
    scale = lax.rsqrt(jnp.sum(wide * wide, axis=1, keepdims=True) / feature + 1e-06)
    factor = jnp.broadcast_to(weight[...], (128, tokens)).T[:, 0:1]

    pl.semaphore_wait(barrier, experts * members + experts)

    def remote(src, dst, send, recv, **place):
        where = {"section": s, "node": n, "local": l}
        where.update(place)
        return pltpu.make_async_remote_copy(
            src_ref=src, dst_ref=dst, send_sem=send, recv_sem=recv, device_id=where, device_id_type=MESH
        )

    def columns(c):
        return pl.ds(pl.multiple_of(c * CHUNK, CHUNK), CHUNK)

    def ids_copy():
        return remote(ids, ids_in, y_send.at[0], y_recv.at[0], section=before)

    def gain_copy():
        return remote(gain, gain_in, y_send.at[1], y_recv.at[1], section=before)

    def rows_copy():
        return remote(prev, rows, y_send.at[2], y_recv.at[2], section=after)

    class Part:
        def __init__(self, p):
            self.p, self.slots, self.group = p, pool[p], members * pool[p]
            (self.sel, self.sel_t, self.packed, self.arrived, self.total, self.hidden, self.results, self.returned,
             self.z_send, self.z_recv, self.g_send, self.g_recv, self.f_send, self.f_recv,
             self.h_send, self.h_recv, self.k_send, self.k_recv, self.r_send, self.r_recv) = parts[p]

        def z_copy(self, c, k):
            node = lax.rem(n + k, experts)
            return remote(
                self.packed.at[c, node], self.arrived.at[c, n, l], self.z_send.at[c, k], self.z_recv.at[c, k],
                section=after, node=node,
            )

        def g_copy(self, c, m):
            block = self.arrived.at[c, :, l]
            peer = sibling if m == 0 else lax.rem(l + 2 * m, members)
            return remote(block, block, self.g_send.at[c, m], self.g_recv.at[c, m], local=peer)

        def f_copy(self, c, m):
            block = self.arrived.at[c, :, lax.rem(l + members - 2 * m, members)]
            return remote(block, block, self.f_send.at[c, m], self.f_recv.at[c, m], local=sibling)

        def h_copy(self, k, m):
            block = self.hidden.at[lax.rem(n + k, experts), l]
            peer = sibling if m == 0 else lax.rem(l + 2 * m, members)
            return remote(block, block, self.h_send.at[k, m], self.h_recv.at[k, m], local=peer)

        def k_copy(self, k, m):
            block = self.hidden.at[lax.rem(n + k, experts), lax.rem(l + members - 2 * m, members)]
            return remote(block, block, self.k_send.at[k, m], self.k_recv.at[k, m], local=sibling)

        def r_copy(self, k, m):
            node, local = lax.rem(n + k, experts), lax.rem(l + m, members)
            if k == 0 and m == 0:
                return pltpu.make_async_copy(self.results.at[n, l], self.returned.at[n, l], self.r_recv.at[0, 0])
            return remote(
                self.results.at[node, local], self.returned.at[n, l], self.r_send.at[k, m], self.r_recv.at[k, m],
                node=node, local=local,
            )

        def dispatch(self, c):
            if self.p == 0:
                normed = (
                    prev[:, columns(c)].astype(jnp.float32) * scale * gain_in[:, columns(c)]
                ).astype(jnp.bfloat16)
                normal[:, columns(c)] = normed
            else:
                normed = normal[:, columns(c)]
            placed = jnp.dot(
                self.sel[0 : experts * self.slots, :], normed, preferred_element_type=jnp.float32
            )
            for e in range(experts):
                for half in range(HALVES):
                    self.packed[c, e, half * self.slots : (half + 1) * self.slots, :] = placed[
                        e * self.slots : (e + 1) * self.slots, half * part : (half + 1) * part
                    ].astype(jnp.bfloat16)
            for k in order:
                self.z_copy(c, k).start()

        def share(self, c):
            for k in range(experts):
                self.z_copy(c, k).wait_recv()
            for m in list(range(1, chips)) + [0]:
                self.g_copy(c, m).start()

        def hand_on(self, c):
            for m in range(1, chips):
                self.g_copy(c, m).wait_recv()
                self.f_copy(c, m).start()

        def multiply(self, c):
            self.g_copy(c, 0).wait_recv()
            for m in range(1, chips):
                self.f_copy(c, m).wait_recv()
            sides = [
                self.arrived[c, :, :, half * self.slots : (half + 1) * self.slots, :]
                .astype(jnp.float32).reshape(experts * self.group, part).astype(jnp.bfloat16)
                for half in range(HALVES)
            ]
            self.total[...] += jnp.dot(
                jnp.concatenate(sides, axis=1), w_in[columns(c), :], preferred_element_type=jnp.float32
            )

        def activate(self):
            for k in order:
                node = lax.rem(n + k, experts)
                span = pl.ds(pl.multiple_of(node * self.group, 16), self.group)
                gate, upper = self.total[span, 0:units], self.total[span, units : 2 * units]
                self.hidden[node, l] = (gate / (1.0 + jnp.exp(-gate)) * upper).astype(jnp.bfloat16)
                for m in list(range(1, chips)) + [0]:
                    self.h_copy(k, m).start()

        def pass_hidden(self, k):
            for m in range(1, chips):
                self.h_copy(k, m).wait_recv()
                self.k_copy(k, m).start()

        def give_back(self, k):
            node = lax.rem(n + k, experts)
            self.h_copy(k, 0).wait_recv()
            for m in range(1, chips):
                self.k_copy(k, m).wait_recv()
            inner = jnp.concatenate([self.hidden[node, j] for j in range(members)], axis=1)
            made = jnp.dot(inner, w_out[...], preferred_element_type=jnp.float32)
            for j in range(members):
                for t in range(tiles):
                    self.results[node, j, t * self.slots : (t + 1) * self.slots, 0 : ends[t]] = made[
                        j * self.slots : (j + 1) * self.slots, t * 128 : t * 128 + ends[t]
                    ].astype(jnp.bfloat16)
            for m in range(members):
                self.r_copy(k, m).start()

        def collect(self):
            for k in order:
                for m in range(members):
                    if k == 0 and m == 0:
                        self.r_copy(k, m).wait()
                    else:
                        self.r_copy(k, m).wait_recv()

        def picked(self, j):
            table = jnp.concatenate(
                [
                    jnp.concatenate(
                        [
                            self.returned[e, j, t * self.slots : (t + 1) * self.slots, 0 : ends[t]].astype(jnp.float32)
                            for t in range(tiles)
                        ],
                        axis=1,
                    )
                    for e in range(experts)
                ],
                axis=0,
            ).astype(jnp.bfloat16)
            return jnp.dot(self.sel_t[:, 0 : experts * self.slots], table, preferred_element_type=jnp.float32)

        def settle(self):
            @pl.loop(0, chunks)
            def _(c):
                for k in range(experts):
                    self.z_copy(c, k).wait_send()
                for m in range(chips):
                    self.g_copy(c, m).wait_send()
                for m in range(1, chips):
                    self.f_copy(c, m).wait_send()

            for k in range(experts):
                for m in range(chips):
                    self.h_copy(k, m).wait_send()
                for m in range(1, chips):
                    self.k_copy(k, m).wait_send()
                for m in range(members):
                    if k or m:
                        self.r_copy(k, m).wait_send()

    first, second = Part(0), Part(1)
    ids_copy().start()
    gain_copy().start()
    ids_copy().wait_recv()
    for p, spread in enumerate(spreads(ids_in[...])):
        parts[p][0][...] = spread.T.astype(jnp.bfloat16)
    gain_copy().wait_recv()

    pl.loop(0, chunks)(first.dispatch)

    @pl.loop(0, chunks)
    def _(step):
        second.dispatch(step)
        first.share(step)

        @pl.when(step >= 1)
        def _():
            first.hand_on(step - 1)

        @pl.when(step == 2)
        def _():
            for load in loads:
                load.wait()

        @pl.when(step >= 2)
        def _():
            first.multiply(step - 2)

    early = chunks // 3
    later = 2 * early
    pl.loop(0, early)(second.share)
    first.hand_on(chunks - 1)
    first.multiply(chunks - 2)
    pl.loop(early, later)(second.share)
    first.multiply(chunks - 1)
    first.activate()
    rows_copy().start()
    pl.loop(later, chunks - 1)(second.share)
    pl.loop(0, later)(second.hand_on)
    for i, k in enumerate(order):
        first.pass_hidden(k)
        if i == 0:
            second.share(chunks - 1)
        if i:
            first.give_back(order[i - 1])
        pl.loop(i * later // experts, (i + 1) * later // experts)(second.multiply)
        if i == experts - 2:
            pl.loop(later, chunks)(second.hand_on)
    first.give_back(order[-1])
    pl.loop(later, chunks)(second.multiply)
    second.activate()
    second.pass_hidden(order[0])
    for i, k in enumerate(order):
        if i + 1 < experts:
            second.pass_hidden(order[i + 1])
        second.give_back(k)
    rows_copy().wait_recv()
    first.collect()
    for j in range(members):
        span = slice(j * width, (j + 1) * width)
        mid[:, span] = rows[:, span].astype(jnp.float32) + first.picked(j) * factor
    second.collect()
    for j in range(members):
        span = slice(j * width, (j + 1) * width)
        out[:, span] = (mid[:, span] + second.picked(j) * factor).astype(jnp.bfloat16)

    ids_copy().wait_send()
    gain_copy().wait_send()
    rows_copy().wait_send()
    first.settle()
    second.settle()


def per_device(sections, experts, members, prev_rows, expert_ids, route_weight, norm_gain, gate_weight, up_weight, down_weight):
    prev = prev_rows[0]
    tokens, feature = prev.shape
    capacity = 5 * tokens * expert_ids.shape[2] // (4 * experts)
    slots = -(-capacity // 8) * 8
    units, width = gate_weight.shape[3], down_weight.shape[3]
    chunks, chips = feature // CHUNK, members // 2
    bf16, f32 = jnp.bfloat16, jnp.float32
    dma = pltpu.SemaphoreType.DMA
    vmem, anywhere = pl.BlockSpec(memory_space=pltpu.VMEM), pl.BlockSpec(memory_space=pl.ANY)
    scratch = [
        pltpu.VMEM((tokens, feature), bf16),
        pltpu.VMEM((tokens, feature), bf16),
        pltpu.VMEM((1, tokens), jnp.int32),
        pltpu.VMEM((1, feature), f32),
        pltpu.VMEM((tokens, feature), f32),
        pltpu.VMEM((feature, 2 * units), bf16),
        pltpu.VMEM((members * units, width), bf16),
        dma((3,)),
        dma((3,)), dma((3,)),
    ]
    for some in split(slots):
        lines = -(-(-(-width // 128) * some) // 16) * 16
        group = members * some
        padded = -(-(experts * some) // 128) * 128
        scratch += [
            pltpu.VMEM((padded, tokens), bf16),
            pltpu.VMEM((tokens, padded), bf16),
            pltpu.VMEM((chunks, experts, HALVES * some, CHUNK // HALVES), bf16),
            pltpu.VMEM((chunks, experts, members, HALVES * some, CHUNK // HALVES), bf16),
            pltpu.VMEM((experts * group, 2 * units), f32),
            pltpu.VMEM((experts, members, group, units), bf16),
            pltpu.VMEM((experts, members, lines, 128), bf16),
            pltpu.VMEM((experts, members, lines, 128), bf16),
            dma((chunks, experts)), dma((chunks, experts)),
            dma((chunks, chips)), dma((chunks, chips)),
            dma((chunks, chips)), dma((chunks, chips)),
            dma((experts, chips)), dma((experts, chips)),
            dma((experts, chips)), dma((experts, chips)),
            dma((experts, members)), dma((experts, members)),
        ]
    mixed = pl.pallas_call(
        functools.partial(kernel, sections, experts, members, slots),
        out_shape=jax.ShapeDtypeStruct((tokens, feature), bf16),
        in_specs=[vmem] * 4 + [anywhere] * 3,
        out_specs=vmem,
        scratch_shapes=scratch,
        compiler_params=pltpu.CompilerParams(
            collective_id=0, has_side_effects=True, vmem_limit_bytes=56 * 1024 * 1024
        ),
    )(
        prev, expert_ids[0].reshape(1, tokens), route_weight[0].reshape(1, tokens), norm_gain,
        gate_weight[0, 0], up_weight[0, 0], down_weight[0, 0],
    )
    return mixed[None]


def solution(mesh):
    placed = (
        P("section", ("node", "local"), None),
        P("section", ("node", "local"), None),
        P("section", ("node", "local"), None),
        P("section", None),
        P("section", "node", None, "local"),
        P("section", "node", None, "local"),
        P("section", "node", None, "local"),
    )
    sizes = mesh.shape
    return jax.shard_map(
        functools.partial(per_device, sizes["section"], sizes["node"], sizes["local"]),
        mesh=mesh,
        in_specs=placed,
        out_specs=P("section", ("node", "local"), None),
        check_vma=False,
    )
```

```python
import functools

import jax
import jax.numpy as jnp
from jax import lax
from jax.experimental import pallas as pl
from jax.experimental.pallas import tpu as pltpu
from jax.sharding import PartitionSpec as P

MESH = pl.DeviceIdType.MESH
HALVES = 2
FLYING = 3
CHUNK = 512


def split(slots):
    first = 8 * -(-slots // 16)
    return (first, slots - first)


def kernel(sections, experts, members, slots, prev, ids, weight, gain, w_gate, w_up, w_down, out, *scratch):
    rows, normal, ids_in, gain_in, mid, w_in, w_out, w_sem, y_send, y_recv = scratch[:10]
    own = (len(scratch) - 10) // 2
    parts = [scratch[10 : 10 + own], scratch[10 + own :]]
    s, n, l = lax.axis_index("section"), lax.axis_index("node"), lax.axis_index("local")
    tokens, feature = prev.shape
    chunks = feature // CHUNK
    part = CHUNK // HALVES
    units = w_gate.shape[1]
    width = w_down.shape[1]
    tiles = -(-width // 128)
    ends = [min(128, width - 128 * t) for t in range(tiles)]
    chips = members // 2
    sibling = l + 1 - 2 * lax.rem(l, 2)
    order = sorted(range(experts), key=lambda k: -min(k, experts - k))

    loads = [
        pltpu.make_async_copy(w_gate, w_in.at[:, pl.ds(0, units)], w_sem.at[0]),
        pltpu.make_async_copy(w_up, w_in.at[:, pl.ds(units, units)], w_sem.at[1]),
        pltpu.make_async_copy(w_down, w_out, w_sem.at[2]),
    ]
    for load in loads:
        load.start()

    barrier = pltpu.get_barrier_semaphore()
    after, before = lax.rem(s + 1, sections), lax.rem(s + sections - 1, sections)
    pl.semaphore_signal(barrier, inc=1, device_id={"section": after, "node": n, "local": l}, device_id_type=MESH)
    for k in range(experts):
        node = lax.rem(n + k, experts)
        pl.semaphore_signal(barrier, inc=1, device_id={"section": before, "node": node, "local": l}, device_id_type=MESH)
        for m in range(members):
            if k or m:
                place = {"section": s, "node": node, "local": lax.rem(l + m, members)}
                pl.semaphore_signal(barrier, inc=1, device_id=place, device_id_type=MESH)

    pool = split(slots)

    def spreads(row):
        chosen = jnp.broadcast_to(row.astype(jnp.float32), (128, tokens)).T
        lanes = lax.broadcasted_iota(jnp.int32, (tokens, 128), 1).astype(jnp.float32)
        onehot = jnp.where(chosen == lanes, 1.0, 0.0)
        earlier = lax.broadcasted_iota(jnp.int32, (tokens, tokens), 1) < lax.broadcasted_iota(
            jnp.int32, (tokens, tokens), 0
        )
        counts = jnp.dot(
            jnp.where(earlier, 1.0, 0.0).astype(jnp.bfloat16), onehot.astype(jnp.bfloat16),
            preferred_element_type=jnp.float32,
        )
        slot = jnp.sum(counts * onehot, axis=1, keepdims=True)
        made = []
        for p in range(2):
            local_slot = slot - (pool[0] if p else 0)
            inside = jnp.logical_and(local_slot >= 0, local_slot < pool[p])
            target = jnp.where(inside, chosen[:, 0:1] * pool[p] + local_slot, -1.0)
            places = lax.broadcasted_iota(jnp.int32, (tokens, parts[p][0].shape[0]), 1).astype(jnp.float32)
            made.append(jnp.where(target == places, 1.0, 0.0))
        return made

    for p, spread in enumerate(spreads(ids[...])):
        parts[p][1][...] = spread.astype(jnp.bfloat16)
        parts[p][4][...] = jnp.zeros_like(parts[p][4])
    wide = prev[...].astype(jnp.float32)
    scale = lax.rsqrt(jnp.sum(wide * wide, axis=1, keepdims=True) / feature + 1e-06)
    factor = jnp.broadcast_to(weight[...], (128, tokens)).T[:, 0:1]

    pl.semaphore_wait(barrier, experts * members + experts)

    def remote(src, dst, send, recv, **place):
        where = {"section": s, "node": n, "local": l}
        where.update(place)
        return pltpu.make_async_remote_copy(
            src_ref=src, dst_ref=dst, send_sem=send, recv_sem=recv, device_id=where, device_id_type=MESH
        )

    def columns(c):
        return pl.ds(pl.multiple_of(c * CHUNK, CHUNK), CHUNK)

    def ids_copy():
        return remote(ids, ids_in, y_send.at[0], y_recv.at[0], section=before)

    def gain_copy():
        return remote(gain, gain_in, y_send.at[1], y_recv.at[1], section=before)

    def rows_copy():
        return remote(prev, rows, y_send.at[2], y_recv.at[2], section=after)

    class Part:
        def __init__(self, p):
            self.p, self.slots, self.group = p, pool[p], members * pool[p]
            (self.sel, self.sel_t, self.packed, self.arrived, self.total, self.hidden, self.results, self.returned,
             self.z_send, self.z_recv, self.g_send, self.g_recv, self.f_send, self.f_recv,
             self.h_send, self.h_recv, self.k_send, self.k_recv, self.r_send, self.r_recv) = parts[p]

        def z_copy(self, c, k):
            node = lax.rem(n + k, experts)
            return remote(
                self.packed.at[c, node], self.arrived.at[c, n, l], self.z_send.at[c, k], self.z_recv.at[c, k],
                section=after, node=node,
            )

        def g_copy(self, c, m):
            block = self.arrived.at[c, :, l]
            peer = sibling if m == 0 else lax.rem(l + 2 * m, members)
            return remote(block, block, self.g_send.at[c, m], self.g_recv.at[c, m], local=peer)

        def f_copy(self, c, m):
            block = self.arrived.at[c, :, lax.rem(l + members - 2 * m, members)]
            return remote(block, block, self.f_send.at[c, m], self.f_recv.at[c, m], local=sibling)

        def h_copy(self, k, m):
            block = self.hidden.at[lax.rem(n + k, experts), l]
            peer = sibling if m == 0 else lax.rem(l + 2 * m, members)
            return remote(block, block, self.h_send.at[k, m], self.h_recv.at[k, m], local=peer)

        def k_copy(self, k, m):
            block = self.hidden.at[lax.rem(n + k, experts), lax.rem(l + members - 2 * m, members)]
            return remote(block, block, self.k_send.at[k, m], self.k_recv.at[k, m], local=sibling)

        def r_copy(self, k, m):
            node, local = lax.rem(n + k, experts), lax.rem(l + m, members)
            if k == 0 and m == 0:
                return pltpu.make_async_copy(self.results.at[n, l], self.returned.at[n, l], self.r_recv.at[0, 0])
            return remote(
                self.results.at[node, local], self.returned.at[n, l], self.r_send.at[k, m], self.r_recv.at[k, m],
                node=node, local=local,
            )

        def dispatch(self, c):
            if self.p == 0:
                normed = (
                    prev[:, columns(c)].astype(jnp.float32) * scale * gain_in[:, columns(c)]
                ).astype(jnp.bfloat16)
                normal[:, columns(c)] = normed
            else:
                normed = normal[:, columns(c)]
            placed = jnp.dot(
                self.sel[0 : experts * self.slots, :], normed, preferred_element_type=jnp.float32
            )
            for e in range(experts):
                for half in range(HALVES):
                    self.packed[c, e, half * self.slots : (half + 1) * self.slots, :] = placed[
                        e * self.slots : (e + 1) * self.slots, half * part : (half + 1) * part
                    ].astype(jnp.bfloat16)
            for k in order:
                self.z_copy(c, k).start()

        def share(self, c):
            for k in range(experts):
                self.z_copy(c, k).wait_recv()
            for m in list(range(1, chips)) + [0]:
                self.g_copy(c, m).start()

        def hand_on(self, c):
            for m in range(1, chips):
                self.g_copy(c, m).wait_recv()
                self.f_copy(c, m).start()

        def multiply(self, c):
            self.g_copy(c, 0).wait_recv()
            for m in range(1, chips):
                self.f_copy(c, m).wait_recv()
            sides = [
                self.arrived[c, :, :, half * self.slots : (half + 1) * self.slots, :]
                .astype(jnp.float32).reshape(experts * self.group, part).astype(jnp.bfloat16)
                for half in range(HALVES)
            ]
            self.total[...] += jnp.dot(
                jnp.concatenate(sides, axis=1), w_in[columns(c), :], preferred_element_type=jnp.float32
            )

        def activate(self):
            for k in order:
                node = lax.rem(n + k, experts)
                span = pl.ds(pl.multiple_of(node * self.group, 16), self.group)
                gate, upper = self.total[span, 0:units], self.total[span, units : 2 * units]
                self.hidden[node, l] = (gate / (1.0 + jnp.exp(-gate)) * upper).astype(jnp.bfloat16)
                for m in list(range(1, chips)) + [0]:
                    self.h_copy(k, m).start()

        def pass_hidden(self, k):
            for m in range(1, chips):
                self.h_copy(k, m).wait_recv()
                self.k_copy(k, m).start()

        def give_back(self, k):
            node = lax.rem(n + k, experts)
            self.h_copy(k, 0).wait_recv()
            for m in range(1, chips):
                self.k_copy(k, m).wait_recv()
            inner = jnp.concatenate([self.hidden[node, j] for j in range(members)], axis=1)
            made = jnp.dot(inner, w_out[...], preferred_element_type=jnp.float32)
            for j in range(members):
                for t in range(tiles):
                    self.results[node, j, t * self.slots : (t + 1) * self.slots, 0 : ends[t]] = made[
                        j * self.slots : (j + 1) * self.slots, t * 128 : t * 128 + ends[t]
                    ].astype(jnp.bfloat16)
            for m in range(members):
                self.r_copy(k, m).start()

        def collect(self):
            for k in order:
                for m in range(members):
                    if k == 0 and m == 0:
                        self.r_copy(k, m).wait()
                    else:
                        self.r_copy(k, m).wait_recv()

        def picked(self, j):
            table = jnp.concatenate(
                [
                    jnp.concatenate(
                        [
                            self.returned[e, j, t * self.slots : (t + 1) * self.slots, 0 : ends[t]].astype(jnp.float32)
                            for t in range(tiles)
                        ],
                        axis=1,
                    )
                    for e in range(experts)
                ],
                axis=0,
            ).astype(jnp.bfloat16)
            return jnp.dot(self.sel_t[:, 0 : experts * self.slots], table, preferred_element_type=jnp.float32)

        def settle(self):
            @pl.loop(0, chunks)
            def _(c):
                for k in range(experts):
                    self.z_copy(c, k).wait_send()
                for m in range(chips):
                    self.g_copy(c, m).wait_send()
                for m in range(1, chips):
                    self.f_copy(c, m).wait_send()

            for k in range(experts):
                for m in range(chips):
                    self.h_copy(k, m).wait_send()
                for m in range(1, chips):
                    self.k_copy(k, m).wait_send()
                for m in range(members):
                    if k or m:
                        self.r_copy(k, m).wait_send()

    first, second = Part(0), Part(1)
    ids_copy().start()
    gain_copy().start()
    ids_copy().wait_recv()
    for p, spread in enumerate(spreads(ids_in[...])):
        parts[p][0][...] = spread.T.astype(jnp.bfloat16)
    gain_copy().wait_recv()

    pl.loop(0, FLYING)(first.dispatch)

    @pl.loop(0, chunks)
    def _(step):
        first.share(step)

        @pl.when(step + FLYING < chunks)
        def _():
            first.dispatch(step + FLYING)

        @pl.when(step + FLYING >= chunks)
        def _():
            second.dispatch(step + FLYING - chunks)

        @pl.when(step >= 2)
        def _():
            first.hand_on(step - 2)

        @pl.when(step == 3)
        def _():
            for load in loads:
                load.wait()

        @pl.when(step >= 3)
        def _():
            first.multiply(step - 3)

    def move(c):
        second.share(c)

        @pl.when(c + FLYING + 1 < chunks)
        def _():
            second.dispatch(c + FLYING + 1)

    early = chunks // 3
    later = 2 * early
    second.dispatch(FLYING)
    first.hand_on(chunks - 2)
    first.multiply(chunks - 3)
    pl.loop(0, early)(move)
    first.hand_on(chunks - 1)
    first.multiply(chunks - 2)
    pl.loop(early, early + 1)(move)
    first.multiply(chunks - 1)
    first.activate()
    pl.loop(early + 1, chunks - 1)(move)
    rows_copy().start()
    pl.loop(0, later)(second.hand_on)
    for i, k in enumerate(order):
        first.pass_hidden(k)
        if i == 0:
            second.share(chunks - 1)
        if i:
            first.give_back(order[i - 1])
        pl.loop(i * later // experts, (i + 1) * later // experts)(second.multiply)
        if i == experts - 2:
            pl.loop(later, chunks)(second.hand_on)
    first.give_back(order[-1])
    pl.loop(later, chunks)(second.multiply)
    second.activate()
    second.pass_hidden(order[0])
    for i, k in enumerate(order):
        if i + 1 < experts:
            second.pass_hidden(order[i + 1])
        second.give_back(k)
    rows_copy().wait_recv()
    first.collect()
    for j in range(members):
        span = slice(j * width, (j + 1) * width)
        mid[:, span] = rows[:, span].astype(jnp.float32) + first.picked(j) * factor
    second.collect()
    for j in range(members):
        span = slice(j * width, (j + 1) * width)
        out[:, span] = (mid[:, span] + second.picked(j) * factor).astype(jnp.bfloat16)

    ids_copy().wait_send()
    gain_copy().wait_send()
    rows_copy().wait_send()
    first.settle()
    second.settle()


def per_device(sections, experts, members, prev_rows, expert_ids, route_weight, norm_gain, gate_weight, up_weight, down_weight):
    prev = prev_rows[0]
    tokens, feature = prev.shape
    capacity = 5 * tokens * expert_ids.shape[2] // (4 * experts)
    slots = -(-capacity // 8) * 8
    units, width = gate_weight.shape[3], down_weight.shape[3]
    chunks, chips = feature // CHUNK, members // 2
    bf16, f32 = jnp.bfloat16, jnp.float32
    dma = pltpu.SemaphoreType.DMA
    vmem, anywhere = pl.BlockSpec(memory_space=pltpu.VMEM), pl.BlockSpec(memory_space=pl.ANY)
    scratch = [
        pltpu.VMEM((tokens, feature), bf16),
        pltpu.VMEM((tokens, feature), bf16),
        pltpu.VMEM((1, tokens), jnp.int32),
        pltpu.VMEM((1, feature), f32),
        pltpu.VMEM((tokens, feature), f32),
        pltpu.VMEM((feature, 2 * units), bf16),
        pltpu.VMEM((members * units, width), bf16),
        dma((3,)),
        dma((3,)), dma((3,)),
    ]
    for some in split(slots):
        lines = -(-(-(-width // 128) * some) // 16) * 16
        group = members * some
        padded = -(-(experts * some) // 128) * 128
        scratch += [
            pltpu.VMEM((padded, tokens), bf16),
            pltpu.VMEM((tokens, padded), bf16),
            pltpu.VMEM((chunks, experts, HALVES * some, CHUNK // HALVES), bf16),
            pltpu.VMEM((chunks, experts, members, HALVES * some, CHUNK // HALVES), bf16),
            pltpu.VMEM((experts * group, 2 * units), f32),
            pltpu.VMEM((experts, members, group, units), bf16),
            pltpu.VMEM((experts, members, lines, 128), bf16),
            pltpu.VMEM((experts, members, lines, 128), bf16),
            dma((chunks, experts)), dma((chunks, experts)),
            dma((chunks, chips)), dma((chunks, chips)),
            dma((chunks, chips)), dma((chunks, chips)),
            dma((experts, chips)), dma((experts, chips)),
            dma((experts, chips)), dma((experts, chips)),
            dma((experts, members)), dma((experts, members)),
        ]
    mixed = pl.pallas_call(
        functools.partial(kernel, sections, experts, members, slots),
        out_shape=jax.ShapeDtypeStruct((tokens, feature), bf16),
        in_specs=[vmem] * 4 + [anywhere] * 3,
        out_specs=vmem,
        scratch_shapes=scratch,
        compiler_params=pltpu.CompilerParams(
            collective_id=0, has_side_effects=True, vmem_limit_bytes=56 * 1024 * 1024
        ),
    )(
        prev, expert_ids[0].reshape(1, tokens), route_weight[0].reshape(1, tokens), norm_gain,
        gate_weight[0, 0], up_weight[0, 0], down_weight[0, 0],
    )
    return mixed[None]


def solution(mesh):
    placed = (
        P("section", ("node", "local"), None),
        P("section", ("node", "local"), None),
        P("section", ("node", "local"), None),
        P("section", None),
        P("section", "node", None, "local"),
        P("section", "node", None, "local"),
        P("section", "node", None, "local"),
    )
    sizes = mesh.shape
    return jax.shard_map(
        functools.partial(per_device, sizes["section"], sizes["node"], sizes["local"]),
        mesh=mesh,
        in_specs=placed,
        out_specs=P("section", ("node", "local"), None),
        check_vma=False,
    )
```
